32 devices in a mesh: seq: 8 (over z, y), exp: 4 (over x, core).
Axes of the slice: x: 2, y: 2, z: 4, core: 2. Of those that a mesh axis runs over, the one named last changes fastest.
Arguments:
- resid_rows: bfloat16 [4, 32, 3072], P('exp', 'seq'), may hold values from -6 to 6
- query_rows: bfloat16 [4, 32, 3072], P('exp', 'seq'), may hold values from -6 to 6
- key_rows: bfloat16 [4, 1024, 3072], P('exp', 'seq'), may hold values from -6 to 6
- value_rows: bfloat16 [4, 1024, 3072], P('exp', 'seq'), may hold values from -6 to 6
- log_decay: float32 [4, 48, 1024], P('exp', None, 'seq'), may hold values from -1 to 0
- read_pos: int32 [4, 32], P('exp', 'seq'), may hold values from 0 to 1023, as said below
- expert_ids: int32 [4, 32, 2], P('exp', 'seq'), may hold values from 0 to 3, all different within a row; in each aligned block of 4 rows (0 to 3, 4 to 7, ..., all dimensions but the last counted through in order) at most 4 rows name the same one
- pair_order: int32 [4], replicated, may hold values from 0 to 3, each once
- lengths: int32 [4], replicated, may hold values from 1 to 1024
- norm_gain: bfloat16 [3072], replicated, may hold values from 0.5 to 1.5
- router_weight: bfloat16 [3072, 4], replicated, may hold values from -0.109375 to 0.109375
- score_weight: bfloat16 [3072], replicated, may hold values from -0.109375 to 0.109375
- gate_weight: bfloat16 [4, 3072, 9216], P('exp', None, 'seq'), may hold values from -0.109375 to 0.109375
- up_weight: bfloat16 [4, 3072, 9216], P('exp', None, 'seq'), may hold values from -0.109375 to 0.109375
- down_weight: bfloat16 [4, 9216, 3072], P('exp', 'seq'), may hold values from -0.0625 to 0.0625
Outputs:
- pair_loss: float32 [], replicated
- grad_query: float32 [4, 32, 3072], P('exp', 'seq')
- grad_resid: float32 [4, 32, 3072], P('exp', 'seq')
- grad_keys: bfloat16 [4, 1024, 3072], P('exp', 'seq')
- grad_values: bfloat16 [4, 1024, 3072], P('exp', 'seq')
The draws below stay inside these ranges and needn't reach their ends.
Inputs may be any that keep to these rules, and one draw needn't show every extreme that they name: `read_pos`: each aligned block j of 4 entries of a sequence holds strictly increasing positions from j * 128 to (j + 1) * 128 - 1, the last of them being (j + 1) * 128 - 1. `expert_ids`: the two entries of a row differ; in the rows of one device (aligned blocks of 4 rows) no expert is named by more than 4 rows. `pair_order`: each sequence appears once.
All inputs are finite; a program needn't handle non-finite values.
Results may differ from the reference program's by a relative error of at most 0.018.
Values may be sent and summed in bfloat16 or wider, within the bound.
A program may use at most 128 MiB of HBM per device.

```python
import math
import jax
import jax.numpy as jnp
import numpy as np
from jax import lax

D = 3072
FOCUS_CHANNELS = 48
HEAD_DIM = 64
FF = 9216
TOK_DEV = 128
READ_DEV = 4
TEXT_SPAN = 1024
READS = 32
TEXT_TOTAL = 4
EXPERTS = 4
CAP = 4
N_SEQ = 8


def draw_log_decay(key, part):
    boundary_indices = jax.random.split(key, 7)
    group_count = TEXT_SPAN // TOK_DEV
    fast_share = 0.5
    picked = jax.random.uniform(boundary_indices[0], (TEXT_TOTAL, FOCUS_CHANNELS, 1))
    fast_rate = jnp.exp(jax.random.uniform(boundary_indices[1], (TEXT_TOTAL, FOCUS_CHANNELS, 1), minval=jnp.log(1.0 / 50.0), maxval=jnp.log(1.0 / 30.0)))
    slow_rate = jnp.exp(jax.random.uniform(boundary_indices[2], (TEXT_TOTAL, FOCUS_CHANNELS, 1), minval=jnp.log(0.05 / TEXT_SPAN), maxval=jnp.log(0.6 / TEXT_SPAN)))
    forgetting_speed = jnp.where(picked < fast_share, fast_rate, slow_rate)
    block_factor = jnp.exp(jax.random.uniform(boundary_indices[3], (TEXT_TOTAL, FOCUS_CHANNELS, group_count), minval=-0.7, maxval=0.7))
    scatter_breadth = jnp.repeat(block_factor, TOK_DEV, axis=2)
    rough_guess = jax.random.uniform(boundary_indices[4], (TEXT_TOTAL, FOCUS_CHANNELS, TEXT_SPAN), minval=0.5, maxval=1.5)
    period_flag = jax.random.uniform(boundary_indices[5], (TEXT_TOTAL, FOCUS_CHANNELS, TEXT_SPAN)) < 2.0 / TEXT_SPAN
    period_span = jnp.log(jax.random.uniform(boundary_indices[6], (TEXT_TOTAL, FOCUS_CHANNELS, TEXT_SPAN), minval=0.5, maxval=0.8))
    return (-forgetting_speed * scatter_breadth * rough_guess + jnp.where(period_flag, period_span, 0.0)).astype(jnp.float32)


def draw_read_pos(key, part):
    group_count = TEXT_SPAN // TOK_DEV
    boundary_indices = jax.random.split(key, TEXT_TOTAL * group_count)

    def choose_rows(sub_key):
        shuffled = jax.random.permutation(sub_key, TOK_DEV - 1)
        return jnp.sort(shuffled[:READ_DEV - 1]).astype(jnp.int32)
    picked = jax.vmap(choose_rows)(boundary_indices).reshape(TEXT_TOTAL, group_count, READ_DEV - 1)
    closing = jnp.full((TEXT_TOTAL, group_count, 1), TOK_DEV - 1, jnp.int32)
    inside = jnp.concatenate([picked, closing], axis=2)
    offset = (jnp.arange(group_count, dtype=jnp.int32) * TOK_DEV)[None, :, None]
    return (inside + offset).reshape(TEXT_TOTAL, READS).astype(jnp.int32)


def touch_ends(values, own_key, least, high):
    longest = values.shape.index(max(values.shape))
    spots = []
    for shift in (0, 1):
        where = [jax.random.randint(jax.random.fold_in(own_key, axis), (), 0, length) for axis, length in enumerate(values.shape)]
        where[longest] = (where[longest] + shift) % values.shape[longest]
        spots.append(tuple(where))
    return values.at[spots[0]].set(least).at[spots[1]].set(high)


def level_of(key, shape, cuts, least, high):
    factor_of, own = 1.0, jax.random.fold_in(key, 6)
    for position, parts in cuts:
        steps = jnp.exp(jax.random.uniform(jax.random.fold_in(own, position), (parts,), jnp.float32, least / len(cuts), high / len(cuts)))
        factor_of = factor_of * jnp.repeat(steps, shape[position] // parts).reshape([-1 if axis == position else 1 for axis in range(len(shape))])
    return factor_of


def assign_block(rng, own, number, rows, number_of, top, bound, slope):
    order = jax.random.permutation(rng, number_of)
    crowded, usual = shares(number_of, rows * top, bound, slope, True), shares(number_of, rows * top, bound, slope, False)
    places = jnp.arange(number_of)

    def named(sizes, turn):
        used = int((sizes > 0).sum())
        fixed = max(1, used // 4)
        passed = fixed + (places - fixed + turn * (used - fixed)) % max(1, number_of - fixed)
        return jnp.zeros((number_of,), jnp.int32).at[order[jnp.where(places < fixed, places, passed)]].set(jnp.asarray(sizes, jnp.int32))

    sizes = jnp.where(number % 4 == 0, named(crowded, number // 4), named(usual, number - number // 4 - 1))
    mixed = jax.random.permutation(jax.random.fold_in(own, 3), number_of)
    source_of, taker = mixed[0:number_of // 2 * 2:2], mixed[1:number_of // 2 * 2:2]
    room = jnp.minimum(sizes[source_of] - 1, bound - sizes[taker]) // 2
    room = jnp.where((source_of == order[0]) | (taker == order[0]) | (sizes[taker] == 0), 0, jnp.maximum(room, 0))
    passed = jax.random.randint(jax.random.fold_in(own, 4), (number_of // 2,), 0, 1 << 20) % (room + 1)
    sizes = sizes.at[source_of].add(-passed).at[taker].add(passed)
    members = jnp.searchsorted(jnp.cumsum(sizes), jnp.arange(rows * top), side="right").astype(jnp.int32)
    table = members.reshape(top, rows).T
    table = table[jax.random.permutation(jax.random.fold_in(own, 1), rows)]
    turn = jax.random.randint(jax.random.fold_in(own, 2), (rows, 1), 0, top)
    return jnp.take_along_axis(table, (jnp.arange(top)[None, :] + turn) % top, axis=1)


def shares(amount, total, limit, slope, full):
    portions = [(1 << 20) // math.isqrt(rank ** slope) + 1 for rank in range(1, amount + 1)]
    largest = limit if full else min(limit, max(-(-total // amount), total * portions[0] // sum(portions)))
    least = 1 if total - largest >= amount - 1 else 0
    holding, rest = [largest] + [least] * (amount - 1), total - largest - least * (amount - 1)
    while rest > 0:
        movable = [i for i in range(1, amount) if holding[i] < largest] or [i for i in range(1, amount) if holding[i] < limit]
        whole, left = sum([portions[i] for i in movable]), rest
        for i in movable:
            more = min(limit - holding[i], max(1, left * portions[i] // whole), rest)
            holding[i] = holding[i] + more
            rest = rest - more
    return np.array(holding)


def normal_values(key, dims, width, bound, shards=(), kind=jnp.bfloat16):
    result = width * jax.random.normal(key, dims, jnp.float32)
    if shards:
        result = result * level_of(key, dims, shards, -0.22, 0.18)
    return jnp.clip(result, -bound, bound).astype(kind)


def setup_inputs(seed: int = 0) -> dict:
    seeds = jax.random.split(jax.random.key(seed), 16)
    resid_rows = normal_values(seeds[0], (TEXT_TOTAL, READS, D), 1.0, 6.0, ((0, 4), (1, 8)))
    query_rows = normal_values(seeds[1], (TEXT_TOTAL, READS, D), 1.0, 6.0, ((0, 4), (1, 8)))
    key_rows = normal_values(seeds[2], (TEXT_TOTAL, TEXT_SPAN, D), 1.0, 6.0, ((0, 4), (1, 8)))
    value_rows = normal_values(seeds[3], (TEXT_TOTAL, TEXT_SPAN, D), 1.0, 6.0, ((0, 4), (1, 8)))
    log_decay = draw_log_decay(jax.random.fold_in(seeds[15], 71), 0)
    read_pos = draw_read_pos(jax.random.fold_in(seeds[15], 71), 0)
    expert_ids_keys = jax.random.split(jax.random.fold_in(seeds[6], 1), TEXT_TOTAL * READS // READ_DEV)
    expert_ids_turns = jax.random.permutation(jax.random.fold_in(seeds[6], 3), TEXT_TOTAL * READS // READ_DEV)
    expert_ids = jax.vmap(lambda own, number: assign_block(jax.random.fold_in(seeds[6], 2), own, number, READ_DEV, EXPERTS, 2, CAP, 1))(expert_ids_keys, expert_ids_turns).reshape((TEXT_TOTAL, READS, 2))
    pair_order = jax.random.permutation(seeds[7], TEXT_TOTAL).astype(jnp.int32)
    lengths = touch_ends(jax.random.randint(seeds[8], (TEXT_TOTAL,), 1, TEXT_SPAN + 1), jax.random.fold_in(seeds[8], 1), 1, TEXT_SPAN).astype(jnp.int32)
    norm_gain = jnp.clip(1.0 + 0.1 * jax.random.normal(seeds[9], (D,), jnp.float32), 0.5, 1.5).astype(jnp.bfloat16)
    router_weight = normal_values(seeds[10], (D, EXPERTS), D ** -0.5, 0.109375)
    score_weight = normal_values(seeds[11], (D,), D ** -0.5, 0.109375)
    gate_weight = normal_values(seeds[12], (EXPERTS, D, FF), D ** -0.5, 0.109375, ((0, 4), (2, 8)))
    up_weight = normal_values(seeds[13], (EXPERTS, D, FF), D ** -0.5, 0.109375, ((0, 4), (2, 8)))
    down_weight = normal_values(seeds[14], (EXPERTS, FF, D), FF ** -0.5, 0.0625, ((0, 4), (1, 8)))
    return dict(resid_rows=resid_rows, query_rows=query_rows, key_rows=key_rows, value_rows=value_rows, log_decay=log_decay, read_pos=read_pos, expert_ids=expert_ids, pair_order=pair_order, lengths=lengths, norm_gain=norm_gain, router_weight=router_weight, score_weight=score_weight, gate_weight=gate_weight, up_weight=up_weight, down_weight=down_weight)


PRECISE = lax.Precision.HIGHEST
EPSILON = 1e-06
LENGTH_WEIGHT = 4.0
SCORE_SCALE = 256.0

def readout_weights(cumulated, places):
    positions = jnp.arange(cumulated.shape[1], dtype=jnp.int32)
    one_hot = (places[:, None] == positions[None, :]).astype(jnp.float32)
    at_read = jnp.dot(cumulated, one_hot.T, precision=PRECISE)
    allowed = positions[None, :] <= places[:, None]
    exponent = jnp.where(allowed[None], at_read[:, :, None] - cumulated[:, None, :], -1e+30)
    return (at_read, jnp.exp(exponent))

def preference_loss(rewards, pair_order, lengths, total_length):
    count = rewards.shape[0]
    ordering = (pair_order[:, None] == jnp.arange(count, dtype=jnp.int32)[None, :]).astype(jnp.float32)
    ranked = jnp.dot(ordering, rewards, precision=PRECISE).reshape(count // 2, 2)
    fitted = jnp.mean(jax.nn.softplus(ranked[:, 1] - ranked[:, 0]))
    share = lengths.astype(jnp.float32) / total_length
    scatter_breadth = jnp.mean((rewards - jnp.mean(rewards)) * (share - jnp.mean(share)))
    return fitted + LENGTH_WEIGHT * scatter_breadth * scatter_breadth

def group_terms(key_group, value_group, decay_group, query_group, place_group, offset):
    cumulated = jnp.cumsum(decay_group, axis=1)
    tail_decay = jnp.exp(cumulated[:, -1:] - cumulated).T[:, :, None]
    own_state = jnp.einsum('thi,thj->hij', key_group * tail_decay, value_group, precision=PRECISE)
    at_read, weight = readout_weights(cumulated, place_group - offset)
    lift = jnp.exp(at_read).T[:, :, None]
    query_key = jnp.einsum('rhi,thi->hrt', query_group.astype(jnp.bfloat16), key_group.astype(jnp.bfloat16), preferred_element_type=jnp.float32) / HEAD_DIM
    return (jnp.exp(cumulated[:, -1]), tail_decay, own_state, lift, weight, query_key)

def split_sequence(query_seq, key_seq, value_seq, decay_seq, place_seq):
    key_groups = key_seq.astype(jnp.float32).reshape(N_SEQ, TOK_DEV, FOCUS_CHANNELS, HEAD_DIM)
    value_groups = value_seq.astype(jnp.float32).reshape(N_SEQ, TOK_DEV, FOCUS_CHANNELS, HEAD_DIM)
    query_groups = query_seq.astype(jnp.float32).reshape(N_SEQ, READ_DEV, FOCUS_CHANNELS, HEAD_DIM)
    decay_groups = decay_seq.reshape(FOCUS_CHANNELS, N_SEQ, TOK_DEV).transpose(1, 0, 2)
    place_groups = place_seq.reshape(N_SEQ, READ_DEV)
    offsets = jnp.arange(N_SEQ, dtype=jnp.int32) * TOK_DEV
    return (key_groups, value_groups, decay_groups, query_groups, place_groups, offsets)

def seq_forward(packed):
    groups = split_sequence(*packed)

    def advance(state, pieces):
        key_group, value_group, decay_group, query_group, place_group, offset = pieces
        decay_total, tail_decay, own_state, lift, weight, query_key = group_terms(key_group, value_group, decay_group, query_group, place_group, offset)
        attended = jnp.einsum('hrt,thj->rhj', weight * query_key, value_group, precision=PRECISE)
        attended = attended + lift * jnp.einsum('rhi,hij->rhj', query_group, state, precision=PRECISE) / HEAD_DIM
        return (decay_total[:, None, None] * state + own_state, (attended, state))
    start = jnp.zeros((FOCUS_CHANNELS, HEAD_DIM, HEAD_DIM), jnp.float32)
    _, (attended, states) = lax.scan(advance, start, groups)
    return (attended.reshape(READS, D), states)

def seq_backward(packed):
    query_seq, key_seq, value_seq, decay_seq, place_seq, grad_seq = packed
    _, states = seq_forward((query_seq, key_seq, value_seq, decay_seq, place_seq))
    groups = split_sequence(query_seq, key_seq, value_seq, decay_seq, place_seq)
    grad_groups = grad_seq.astype(jnp.float32).reshape(N_SEQ, READ_DEV, FOCUS_CHANNELS, HEAD_DIM)

    def retreat(suffix, pieces):
        key_group, value_group, decay_group, query_group, place_group, offset, grad_group, state = pieces
        decay_total, tail_decay, own_state, lift, weight, query_key = group_terms(key_group, value_group, decay_group, query_group, place_group, offset)
        grad_dot = jnp.einsum('rhj,thj->hrt', grad_group.astype(jnp.bfloat16), value_group.astype(jnp.bfloat16), preferred_element_type=jnp.float32) / HEAD_DIM
        grad_query = jnp.einsum('hrt,thi->rhi', weight * grad_dot, key_group, precision=PRECISE)
        grad_query = grad_query + lift * jnp.einsum('rhj,hij->rhi', grad_group, state, precision=PRECISE) / HEAD_DIM
        grad_keys = jnp.einsum('hrt,rhi->thi', weight * grad_dot, query_group, precision=PRECISE)
        grad_keys = grad_keys + tail_decay * jnp.einsum('hij,thj->thi', suffix, value_group, precision=PRECISE)
        grad_values = jnp.einsum('hrt,rhj->thj', weight * query_key, grad_group, precision=PRECISE)
        grad_values = grad_values + tail_decay * jnp.einsum('thi,hij->thj', key_group, suffix, precision=PRECISE)
        summary = jnp.einsum('rhi,rhj->hij', query_group * lift, grad_group, precision=PRECISE) / HEAD_DIM
        return (decay_total[:, None, None] * suffix + summary, (grad_query, grad_keys, grad_values))
    start = jnp.zeros((FOCUS_CHANNELS, HEAD_DIM, HEAD_DIM), jnp.float32)
    _, (grad_query, grad_keys, grad_values) = lax.scan(retreat, start, groups + (grad_groups, states), reverse=True)
    return (grad_query.reshape(READS, D), grad_keys.reshape(TEXT_SPAN, D), grad_values.reshape(TEXT_SPAN, D))

def split_sum(lefts, rights):
    left_parts = tuple((matrix.reshape(matrix.shape[0], N_SEQ, -1).transpose(1, 0, 2) for matrix in lefts))
    right_parts = tuple((matrix.reshape(N_SEQ, -1, matrix.shape[1]) for matrix in rights))
    row_count = lefts[0].shape[0]
    col_count = rights[0].shape[1]

    def accumulate(total, pieces):
        left_piece, right_piece = pieces
        partial_term = jnp.zeros((row_count, col_count), jnp.float32)
        for index in range(len(left_piece)):
            partial_term = partial_term + jnp.dot(left_piece[index], right_piece[index], preferred_element_type=jnp.float32)
        rounded = lax.optimization_barrier(partial_term.astype(jnp.bfloat16))
        return (total + rounded.astype(jnp.float32), None)
    total, _ = lax.scan(accumulate, jnp.zeros((row_count, col_count), jnp.float32), (left_parts, right_parts))
    return total.astype(jnp.bfloat16)

def reference(resid_rows, query_rows, key_rows, value_rows, log_decay, read_pos, expert_ids, pair_order, lengths, norm_gain, router_weight, score_weight, gate_weight, up_weight, down_weight):
    attended = lax.map(lambda packed: seq_forward(packed)[0], (query_rows, key_rows, value_rows, log_decay, read_pos))
    row_count = TEXT_TOTAL * READS
    assign_count = 2 * row_count
    block_count = TEXT_TOTAL * N_SEQ
    residual = (resid_rows.astype(jnp.float32) + attended).reshape(row_count, D)
    inverse = lax.rsqrt(lax.optimization_barrier(jnp.mean(residual * residual, axis=1, keepdims=True)) + EPSILON)
    unit_rows = residual * inverse
    gain_float = norm_gain.astype(jnp.float32)
    normed = (unit_rows * gain_float).astype(jnp.bfloat16)
    logits = jnp.dot(normed, router_weight, preferred_element_type=jnp.float32)
    pair_ids = expert_ids.reshape(row_count, 2).astype(jnp.int32)
    picks = (pair_ids[:, :, None] == jnp.arange(EXPERTS, dtype=jnp.int32)[None, None, :]).astype(jnp.float32)
    chosen = jnp.einsum('rke,re->rk', picks, logits, precision=PRECISE)
    first = jax.nn.sigmoid(chosen[:, 0] - chosen[:, 1])
    gates = jnp.stack([first, 1.0 - first], axis=1)
    flat_ids = pair_ids.reshape(assign_count)
    hits = (flat_ids[:, None] == jnp.arange(EXPERTS, dtype=jnp.int32)[None, :]).astype(jnp.int32)
    per_block = hits.reshape(block_count, 2 * READ_DEV, EXPERTS)
    earlier = (jnp.cumsum(per_block, axis=1) - per_block).reshape(assign_count, EXPERTS)
    slot_index = lax.optimization_barrier(jnp.sum(earlier * hits, axis=1)).astype(jnp.int32)
    blocks = jnp.arange(assign_count, dtype=jnp.int32) // (2 * READ_DEV)
    target = (blocks * CAP + slot_index).astype(jnp.int32)
    table = jnp.full((EXPERTS, block_count * CAP), assign_count, jnp.int32)
    table = table.at[flat_ids, target].set(jnp.arange(assign_count, dtype=jnp.int32))
    padded_rows = jnp.concatenate([normed, jnp.zeros((1, D), jnp.bfloat16)], axis=0)

    def project_in(index_row, gate_w, up_w):
        taken = padded_rows[index_row // 2]
        pre_gate = jnp.dot(taken, gate_w, preferred_element_type=jnp.float32)
        pre_up = jnp.dot(taken, up_w, preferred_element_type=jnp.float32)
        return (pre_gate, pre_up)

    def expert_forward(packed):
        index_row, gate_w, up_w, down_w = packed
        pre_gate, pre_up = project_in(index_row, gate_w, up_w)
        activated = (jax.nn.silu(pre_gate) * pre_up).astype(jnp.bfloat16)
        return split_sum((activated,), (down_w,))
    expert_slots = lax.map(expert_forward, (table, gate_weight, up_weight, down_weight))
    expert_out = expert_slots[flat_ids, target].reshape(row_count, 2, D).astype(jnp.float32)
    mixed = residual + lax.optimization_barrier(jnp.sum(gates[:, :, None] * expert_out, axis=1))
    score_float = score_weight.astype(jnp.float32)
    score = jnp.dot(mixed, score_float, precision=PRECISE)
    rewards = lax.optimization_barrier(jnp.mean(score.reshape(TEXT_TOTAL, READS), axis=1))
    pair_loss, d_reward = jax.value_and_grad(preference_loss)(rewards, pair_order, lengths, TEXT_SPAN)
    d_mixed = jnp.repeat(SCORE_SCALE * d_reward, READS)[:, None] * score_float[None, :]
    d_out = (gates[:, :, None] * d_mixed[:, None, :]).astype(jnp.bfloat16)
    d_gates = jnp.einsum('rd,rkd->rk', d_mixed, expert_out, precision=PRECISE)
    d_logit = (d_gates[:, 0] - d_gates[:, 1]) * first * (1.0 - first)
    padded_grads = jnp.concatenate([d_out.reshape(assign_count, D), jnp.zeros((1, D), jnp.bfloat16)], axis=0)

    def expert_backward(packed):
        index_row, gate_w, up_w, down_w = packed
        pre_gate, pre_up = project_in(index_row, gate_w, up_w)
        grads_in = padded_grads[index_row]
        d_act = jnp.dot(grads_in, down_w.T, preferred_element_type=jnp.float32)
        gate_sigmoid = jax.nn.sigmoid(pre_gate)
        d_pre_gate = (d_act * pre_up * gate_sigmoid * (1.0 + pre_gate * (1.0 - gate_sigmoid))).astype(jnp.bfloat16)
        d_pre_up = (d_act * pre_gate * gate_sigmoid).astype(jnp.bfloat16)
        return split_sum((d_pre_gate, d_pre_up), (gate_w.T, up_w.T))
    d_in_slots = lax.map(expert_backward, (table, gate_weight, up_weight, down_weight))
    d_in = d_in_slots[flat_ids, target].reshape(row_count, 2, D).astype(jnp.float32)
    columns = jnp.einsum('rke,de->rkd', picks, router_weight.astype(jnp.float32), precision=PRECISE)
    d_normed = lax.optimization_barrier(jnp.sum(d_in, axis=1)) + d_logit[:, None] * (columns[:, 0] - columns[:, 1])
    d_unit = d_normed * gain_float
    grad_resid = d_mixed + inverse * (d_unit - unit_rows * lax.optimization_barrier(jnp.mean(d_unit * unit_rows, axis=1, keepdims=True)))
    d_attended = grad_resid.astype(jnp.bfloat16).reshape(TEXT_TOTAL, READS, D)
    grad_query, grad_keys, grad_values = lax.map(seq_backward, (query_rows, key_rows, value_rows, log_decay, read_pos, d_attended))
    return (pair_loss, grad_query, grad_resid.reshape(TEXT_TOTAL, READS, D), grad_keys.astype(jnp.bfloat16), grad_values.astype(jnp.bfloat16))
```

```python
import functools

import jax
import jax.numpy as jnp
import numpy as np
from jax import lax
from jax.experimental import pallas as pl
from jax.experimental.pallas import tpu as pltpu
from jax.sharding import PartitionSpec as P

EPSILON = 1e-06
LENGTH_WEIGHT = 4.0
SCORE_SCALE = 256.0
NEGATIVE = -1e30
MESH = pl.DeviceIdType.MESH
F32 = jnp.float32
BF16 = jnp.bfloat16


def nt(a, b, **kw):
    return lax.dot_general(a, b, (((1,), (1,)), ((), ())), preferred_element_type=F32, **kw)


def tn(a, b):
    return lax.dot_general(a, b, (((0,), (0,)), ((), ())), preferred_element_type=F32)


def nn(a, b, **kw):
    return lax.dot_general(a, b, (((1,), (0,)), ((), ())), preferred_element_type=F32, **kw)


def iota(shape, dim):
    return lax.broadcasted_iota(jnp.int32, shape, dim)


def lane_sum(x):
    return jnp.sum(x, axis=1, keepdims=True)


def row_sum(x):
    return jnp.sum(x, axis=0, keepdims=True)


def tile_size(count, best):
    while count % best:
        best //= 2
    return best


def kernel(
    dims,
    q16_ref,
    rows_ref,
    key_ref,
    value_ref,
    decay_ref,
    pos_ref,
    ids_ref,
    order_ref,
    length_ref,
    rt_ref,
    gather_ref,
    spread_ref,
    merge_ref,
    gate_hbm,
    up_hbm,
    down_hbm,
    loss_ref,
    gquery_ref,
    gresid_ref,
    gkeys_ref,
    gvalues_ref,
    w_buf,
    down_buf,
    q_buf,
    info_buf,
    att_send,
    att_recv,
    n_buf,
    meta_buf,
    meta_exp,
    x_buf,
    acc,
    h_buf,
    act_buf,
    v_buf,
    u_buf,
    red_recv,
    red_sum,
    t_send,
    t_recv,
    seq_send,
    seq_recv,
    d_buf,
    gq_send,
    gq_recv,
    qn,
    dn,
    natural,
    w_scr,
    g_scr,
    send_sem,
    recv_sem,
    load_sem,
):
    S, E, R, D, H, TOK, F, Q = dims
    DQ, SR = D // Q, S * R
    NR = E * SR
    HD = D // H
    B = R * Q
    seq, exp = lax.axis_index("seq"), lax.axis_index("exp")
    seq_bits = [1 << b for b in range(S.bit_length() - 1)]
    exp_bits = [1 << b for b in range(E.bit_length() - 1)]
    used = [0]
    sent = []

    def flip(me, bit):
        return me + bit * (1 - 2 * ((me // bit) % 2))

    def push(src, dst, device):
        k = used[0]
        used[0] += 1
        copy = pltpu.make_async_remote_copy(
            src_ref=src,
            dst_ref=dst,
            send_sem=send_sem.at[k],
            recv_sem=recv_sem.at[k],
            device_id=device,
            device_id_type=MESH,
        )
        copy.start()
        sent.append(copy)
        return copy

    def rows_of(index, size):
        return pl.ds(pl.multiple_of(index * size, size), size)

    def share(buf, size):
        out = []
        for k in range(1, S):
            piece = buf.at[rows_of(seq, size)]
            out.append(push(piece, piece, (lax.rem(seq + k, S), exp)))
        return out

    def scatter(src, dst):
        out = []
        for k in range(1, S):
            to = lax.rem(seq + k, S)
            out.append(push(src.at[rows_of(to, B)], dst.at[rows_of(seq, B)], (to, exp)))
        return out

    def arrive(copies):
        for copy in copies:
            copy.wait_recv()

    loads = [
        pltpu.make_async_copy(down_hbm.at[0], down_buf, load_sem.at[0]),
        pltpu.make_async_copy(gate_hbm.at[0], w_buf.at[:, pl.ds(0, F)], load_sem.at[1]),
        pltpu.make_async_copy(up_hbm.at[0], w_buf.at[:, pl.ds(F, F)], load_sem.at[2]),
    ]
    for load in loads:
        load.start()

    barrier = pltpu.get_barrier_semaphore()
    peers = [(lax.rem(seq + k, S), exp) for k in range(1, S)]
    peers += [(seq, flip(exp, bit)) for bit in exp_bits]
    for peer in peers:
        pl.semaphore_signal(barrier, inc=1, device_id=peer, device_id_type=MESH)
    pl.semaphore_wait(barrier, len(peers))

    q_buf[rows_of(seq, B), :] = q16_ref[...]
    q_copies = share(q_buf, B)

    upper = (iota((TOK, TOK), 0) <= iota((TOK, TOK), 1)).astype(F32)
    cum = nn(decay_ref[0], upper, precision=lax.Precision.HIGHEST)
    sub8, lane8 = iota((8, TOK), 0), iota((8, TOK), 1)
    place = jnp.full((8, TOK), TOK - 1, jnp.int32)
    for r in range(R):
        place = jnp.where(sub8 == r, pos_ref[0, r] - seq * TOK, place)
    hot = (lane8 == place).astype(F32)
    marks = nt(hot, cum, precision=lax.Precision.HIGHEST)
    info_buf[rows_of(seq, 8), :] = jnp.zeros((8, 128), F32)
    info_buf[rows_of(seq, 8), 0:H] = marks
    info_copies = share(info_buf, 8)

    loads[0].wait()
    step = tile_size(F, 128)

    def project(i, carry):
        at = pl.multiple_of(i * step, step)
        v_buf[:, pl.ds(at, step)] = nt(rt_ref[...], down_buf[pl.ds(at, step), :])
        return carry

    lax.fori_loop(0, F // step, project, 0)

    arrive(info_copies)
    total = jnp.zeros((1, 128), F32)
    parts, masks = [], []
    lane_r, sub_r = iota((R, TOK), 1), iota((R, TOK), 0)
    own_place = jnp.zeros((R, TOK), jnp.int32)
    for r in range(R):
        own_place = jnp.where(sub_r == r, pos_ref[0, r] - seq * TOK, own_place)
    own_mask = jnp.where(lane_r <= own_place, 0.0, NEGATIVE)
    for j in range(S):
        block = info_buf[j * 8 : (j + 1) * 8, :]
        parts.append(block[0:R] + total)
        masks.append(jnp.where(j == seq, own_mask, jnp.where(j > seq, 0.0, NEGATIVE)))
        total = total + jnp.where(j >= seq, block[R : R + 1], 0.0)
    lifted = jnp.concatenate(parts, axis=0)
    mask = jnp.concatenate(masks, axis=0)

    arrive(q_copies)
    for c in range(Q):
        qn[:, c * DQ : (c + 1) * DQ] = nn(gather_ref[c], q_buf[...])

    group = 128 // HD
    lane = iota((SR, 128), 1)
    slots = [((lane >= g * HD) & (lane < (g + 1) * HD)) for g in range(group)]

    def stacked(x):
        return jnp.concatenate([jnp.where(s, x, 0.0) for s in slots], axis=0).astype(BF16)

    def chosen_lanes(x):
        out = x[0:SR]
        for g in range(1, group):
            out = jnp.where(slots[g], x[g * SR : (g + 1) * SR], out)
        return out

    for p in range(H // group):
        at = slice(p * 128, (p + 1) * 128)
        qk = nt(stacked(qn[:, at]), key_ref[0, :, at]) * (1.0 / HD)
        weight = jnp.concatenate(
            [
                jnp.exp(lifted[:, h : h + 1] - cum[h : h + 1, :] + mask)
                for h in range(p * group, (p + 1) * group)
            ],
            axis=0,
        )
        w_scr[p] = weight
        mixed = (weight * qk).astype(BF16)
        g_scr[p] = mixed
        natural[:, at] = chosen_lanes(nn(mixed, value_ref[0, :, at]))

    def to_blocks(dst):
        out = jnp.zeros((S * B, DQ), F32)
        for c in range(Q):
            out = out + nn(spread_ref[c], natural[:, c * DQ : (c + 1) * DQ].astype(BF16))
        dst[...] = out.astype(BF16)

    def from_blocks(buf):
        return jnp.concatenate([nn(merge_ref[c], buf[...]) for c in range(Q)], axis=1)

    to_blocks(att_send)
    copies = scatter(att_send, att_recv)
    att_recv[rows_of(seq, B), :] = att_send[rows_of(seq, B), :]
    arrive(copies)
    attended = from_blocks(att_recv)
    live = iota((8, 1), 0) < R
    residual = jnp.where(live, rows_ref[...] + attended, 0.0)
    gain = rows_ref[R : R + 1, :]
    score_w = rows_ref[R + 1 : R + 2, :]
    inverse = lax.rsqrt(lane_sum(residual * residual) * (1.0 / D) + EPSILON)
    unit = residual * inverse
    normed = jnp.concatenate([unit * gain, jnp.zeros((8, D), F32)], axis=0).astype(BF16)
    block = jnp.zeros((B, DQ), F32)
    pick = iota((B, 16), 0) - iota((B, 16), 1)
    low = iota((B, 16), 1) < R
    for c in range(Q):
        block = block + nn(
            ((pick == c * R) & low).astype(BF16), normed[:, c * DQ : (c + 1) * DQ]
        )
    n_buf[rows_of(seq, B), :] = block.astype(BF16)
    n_copies = share(n_buf, B)

    logits = nt(normed, rt_ref[...])[0:8]
    sub_l, lane_l = iota((8, 16), 0), iota((8, 16), 1)
    sub_n, lane_n = iota((8, NR), 0), iota((8, NR), 1)
    own_lane = (exp * S + seq) * R
    id0 = jnp.full((8, 16), -1, jnp.int32)
    id1 = jnp.full((8, 16), -1, jnp.int32)
    meta = jnp.zeros((8, NR), F32)
    for r in range(R):
        id0 = jnp.where(sub_l == r, ids_ref[0, r, 0], id0)
        id1 = jnp.where(sub_l == r, ids_ref[0, r, 1], id1)
        here = lane_n == own_lane + r
        meta = jnp.where(here & (sub_n == 0), ids_ref[0, r, 0].astype(F32), meta)
        meta = jnp.where(here & (sub_n == 1), ids_ref[0, r, 1].astype(F32), meta)
    difference = (lane_l == id0).astype(F32) - (lane_l == id1).astype(F32)
    first_own = jax.nn.sigmoid(lane_sum(difference * logits))
    base_own = lane_sum(residual * score_w)
    own_hot = (lane_n == own_lane + sub_n) & (sub_n < R)
    meta = meta + jnp.where(sub_n == 2, row_sum(jnp.where(own_hot, base_own, 0.0)), 0.0)
    meta = meta + jnp.where(sub_n == 3, row_sum(jnp.where(own_hot, first_own, 0.0)), 0.0)
    meta_buf[rows_of(seq, 8), :] = meta
    meta_copies = share(meta_buf, 8)

    arrive(n_copies)
    for c in range(Q):
        x_buf[c, rows_of(exp, SR), :] = nn(gather_ref[c], n_buf[...]).astype(BF16)
    downward = exp_bits[::-1]

    def spread_stage(c, bit):
        held = exp % (2 * bit)
        out = []
        for m in range(E // (2 * bit)):
            piece = x_buf.at[c, rows_of(held + m * 2 * bit, SR)]
            out.append(push(piece, piece, (seq, flip(exp, bit))))
        return out

    stage = [spread_stage(c, downward[0]) for c in range(Q)]
    arrive(meta_copies)
    meta = meta_buf[0:8, :]
    for j in range(1, S):
        meta = meta + meta_buf[j * 8 : (j + 1) * 8, :]

    for bit in downward[1:]:
        following = []
        for c in range(Q):
            arrive(stage[c])
            following.append(spread_stage(c, bit))
        stage = following

    for i, bit in enumerate(downward):
        meta_exp[2 * i] = meta
        copy = push(meta_exp.at[2 * i], meta_exp.at[2 * i + 1], (seq, flip(exp, bit)))
        copy.wait_recv()
        meta = meta + meta_exp[2 * i + 1]

    loads[1].wait()
    loads[2].wait()
    wide = tile_size(2 * F, 768 if (2 * F) % 768 == 0 else 256)
    for c in range(Q):
        arrive(stage[c])

        def grow(i, carry, c=c):
            at = pl.ds(pl.multiple_of(i * wide, wide), wide)
            part = nn(x_buf[c], w_buf[c * DQ : (c + 1) * DQ, at])
            acc[:, at] = part if c == 0 else acc[:, at] + part
            return carry

        lax.fori_loop(0, 2 * F // wide, grow, 0)

    id0_all, id1_all = meta[0:1], meta[1:2]
    base_all, first_all = meta[2:3], meta[3:4]
    mine = exp.astype(F32)
    gate_row = jnp.where(id0_all == mine, first_all, 0.0) + jnp.where(
        id1_all == mine, 1.0 - first_all, 0.0
    )
    v = v_buf[E : E + 1, :]
    sub16, lane16 = iota((16, NR), 0), iota((16, NR), 1)

    def activate(i, carry):
        at = pl.ds(pl.multiple_of(i * 16, 16), 16)
        gate = lane_sum(jnp.where(lane16 == sub16 + i * 16, gate_row, 0.0))
        pre_gate = acc[at, 0:F]
        pre_up = acc[at, F : 2 * F]
        sig = jax.nn.sigmoid(pre_gate)
        silu = pre_gate * sig
        act_buf[at, :] = (silu * pre_up).astype(BF16)
        gv = gate * v
        h_buf[at, 0:F] = (gv * pre_up * sig * (1.0 + pre_gate * (1.0 - sig))).astype(BF16)
        h_buf[at, F : 2 * F] = (gv * silu).astype(BF16)
        return carry

    lax.fori_loop(0, NR // 16, activate, 0)
    v_high = v.astype(BF16).astype(F32)
    sub_v = iota((16, F), 0)
    v_two = jnp.where(sub_v == 0, v_high, jnp.where(sub_v == 1, v - v_high, 0.0)).astype(BF16)
    own_t = row_sum(nt(v_two, act_buf[...]))
    table = jnp.where(sub_n == exp, own_t, 0.0)

    ladder = [(flip(seq, bit), exp) for bit in seq_bits] + [(seq, flip(exp, bit)) for bit in exp_bits]
    climb = []

    def climb_start(table):
        i = len(climb)
        t_send[i] = table
        climb.append(push(t_send.at[i], t_recv.at[i], ladder[i]))

    def climb_end(table):
        i = len(climb) - 1
        climb[i].wait_recv()
        return table + t_recv[i]

    offsets, count = [], E
    reach = 0
    for bit in exp_bits:
        offsets.append(reach)
        count //= 2
        reach += count * SR

    def held_rows(i, m):
        return u_buf, m * SR if i == 0 else offsets[i - 1] + m * SR

    def fold_start(c, i):
        bit = exp_bits[i]
        side = 1 - (exp // bit) % 2
        out = []
        for m in range(E // (2 * bit)):
            if i == 0:
                src = u_buf.at[c, rows_of(2 * m + side, SR)]
            else:
                src = red_sum.at[c, rows_of(offsets[i - 1] // SR + 2 * m + side, SR)]
            dst = red_recv.at[c, pl.ds(offsets[i] + m * SR, SR)]
            out.append(push(src, dst, (seq, flip(exp, bit))))
        return out

    def fold_end(c, i, copies):
        bit = exp_bits[i]
        side = (exp // bit) % 2
        for m, copy in enumerate(copies):
            copy.wait_recv()
            if i == 0:
                own = u_buf[c, rows_of(2 * m + side, SR), :]
            else:
                own = red_sum[c, rows_of(offsets[i - 1] // SR + 2 * m + side, SR), :]
            at = pl.ds(offsets[i] + m * SR, SR)
            red_sum[c, at, :] = (own.astype(F32) + red_recv[c, at, :].astype(F32)).astype(BF16)

    deep = tile_size(DQ, 256)
    folds = {}
    for c in range(Q):
        if c < len(ladder):
            climb_start(table)

        def back(i, carry, c=c):
            at = pl.multiple_of(i * deep, deep)
            u_buf[c, :, pl.ds(at, deep)] = nt(
                h_buf[...], w_buf[pl.ds(c * DQ + at, deep), :]
            ).astype(BF16)
            return carry

        lax.fori_loop(0, DQ // deep, back, 0)
        folds[c, 0] = fold_start(c, 0)
        if c >= 1:
            fold_end(c - 1, 0, folds[c - 1, 0])
            if len(exp_bits) > 1:
                folds[c - 1, 1] = fold_start(c - 1, 1)
        if c < len(ladder):
            table = climb_end(table)
    fold_end(Q - 1, 0, folds[Q - 1, 0])
    if len(exp_bits) > 1:
        folds[Q - 1, 1] = fold_start(Q - 1, 1)
    while len(climb) < len(ladder):
        climb_start(table)
        table = climb_end(table)

    low_e = iota((E, NR), 0).astype(F32)
    picked0 = row_sum(jnp.where(low_e == id0_all, table[0:E], 0.0))
    picked1 = row_sum(jnp.where(low_e == id1_all, table[0:E], 0.0))
    score = base_all + first_all * picked0 + (1.0 - first_all) * picked1
    in_seq = (lane_n >= sub_n * SR) & (lane_n < (sub_n + 1) * SR)
    rewards = lane_sum(jnp.where(in_seq, score, 0.0)) * (1.0 / SR)
    column = iota((8, 1), 0)
    d_reward = jnp.zeros((8, 1), F32)
    fitted = jnp.zeros((1, 1), F32)
    for pair in range(E // 2):
        best, worst = order_ref[2 * pair], order_ref[2 * pair + 1]
        gap = row_sum(
            jnp.where(column == worst, rewards, 0.0) - jnp.where(column == best, rewards, 0.0)
        )
        fitted = fitted + jnp.maximum(gap, 0.0) + jnp.log1p(jnp.exp(-jnp.abs(gap)))
        slope = jax.nn.sigmoid(gap) * (2.0 / E)
        d_reward = d_reward + jnp.where(column == worst, slope, 0.0)
        d_reward = d_reward - jnp.where(column == best, slope, 0.0)
    portion = jnp.zeros((8, 1), F32)
    for i in range(E):
        portion = jnp.where(column == i, length_ref[i].astype(F32) / (TOK * S), portion)
    real = column < E
    spread = jnp.where(real, portion - row_sum(portion) / E, 0.0)
    centred = jnp.where(real, rewards - row_sum(jnp.where(real, rewards, 0.0)) / E, 0.0)
    cov = row_sum(centred * spread) / E
    loss_ref[...] = jnp.broadcast_to(fitted * (2.0 / E) + LENGTH_WEIGHT * cov * cov, (8, 128))
    d_reward = d_reward + (2.0 * LENGTH_WEIGHT / E) * cov * spread
    own_grad = row_sum(jnp.where(column == exp, d_reward, 0.0)) * SCORE_SCALE
    d_logit_row = (picked0 - picked1) * first_all * (1.0 - first_all)
    d_logit = lane_sum(jnp.where(own_hot, d_logit_row, 0.0)) * own_grad

    for i in range(1, len(exp_bits)):
        for c in range(Q):
            fold_end(c, i, folds[c, i])
            if i + 1 < len(exp_bits):
                folds[c, i + 1] = fold_start(c, i + 1)
    out = jnp.zeros((S * B, DQ), F32)
    for c in range(Q):
        out = out + nn(spread_ref[c], red_sum[c, offsets[-1] : offsets[-1] + SR, :])
    seq_send[...] = out.astype(BF16)
    copies = scatter(seq_send, seq_recv)
    seq_recv[rows_of(seq, B), :] = seq_send[rows_of(seq, B), :]
    columns = nn(
        jnp.concatenate([difference, jnp.zeros((8, 16), F32)], axis=0).astype(BF16), rt_ref[...]
    )[0:8]
    arrive(copies)
    d_normed = own_grad * from_blocks(seq_recv) + d_logit * columns
    d_unit = d_normed * gain
    grad_resid = own_grad * score_w + inverse * (
        d_unit - unit * (lane_sum(d_unit * unit) * (1.0 / D))
    )
    grad_resid = jnp.where(live, grad_resid, 0.0)
    gresid_ref[0] = grad_resid[0:R]
    rounded = jnp.concatenate([grad_resid, jnp.zeros((8, D), F32)], axis=0).astype(BF16)
    block = jnp.zeros((B, DQ), F32)
    for c in range(Q):
        block = block + nn(
            ((pick == c * R) & low).astype(BF16), rounded[:, c * DQ : (c + 1) * DQ]
        )
    d_buf[rows_of(seq, B), :] = block.astype(BF16)
    arrive(share(d_buf, B))
    for c in range(Q):
        dn[:, c * DQ : (c + 1) * DQ] = nn(gather_ref[c], d_buf[...])

    for p in range(H // group):
        at = slice(p * 128, (p + 1) * 128)
        d_stack = stacked(dn[:, at])
        grad_dot = nt(d_stack, value_ref[0, :, at]) * (1.0 / HD)
        pulled = (w_scr[p] * grad_dot).astype(BF16)
        natural[:, at] = chosen_lanes(nn(pulled, key_ref[0, :, at]))
        gkeys_ref[0, :, at] = tn(pulled, stacked(qn[:, at])).astype(BF16)
        gvalues_ref[0, :, at] = tn(g_scr[p], d_stack).astype(BF16)
    to_blocks(gq_send)
    copies = scatter(gq_send, gq_recv)
    gq_recv[rows_of(seq, B), :] = gq_send[rows_of(seq, B), :]
    arrive(copies)
    gquery_ref[0] = from_blocks(gq_recv)[0:R]
    for copy in sent:
        copy.wait_send()


def per_device(
    resid_rows,
    query_rows,
    key_rows,
    value_rows,
    log_decay,
    read_pos,
    expert_ids,
    pair_order,
    lengths,
    norm_gain,
    router_weight,
    score_weight,
    gate_weight,
    up_weight,
    down_weight,
):
    S, E = lax.axis_size("seq"), lax.axis_size("exp")
    _, R, D = query_rows.shape
    TOK, H = key_rows.shape[1], log_decay.shape[1]
    F = gate_weight.shape[2]
    extra = -F % 128
    if extra:
        gate_weight = jnp.pad(gate_weight, ((0, 0), (0, 0), (0, extra)))
        up_weight = jnp.pad(up_weight, ((0, 0), (0, 0), (0, extra)))
        down_weight = jnp.pad(down_weight, ((0, 0), (0, extra), (0, 0)))
        F += extra
    Q = 16 // R
    B, DQ, SR = R * Q, D // Q, S * R
    NR = E * SR
    group = 128 // (D // H)

    gather = np.zeros((Q, SR, S * B), np.float32)
    merge = np.zeros((Q, 8, S * B), np.float32)
    for c in range(Q):
        for j in range(S):
            for r in range(R):
                gather[c, j * R + r, j * B + c * R + r] = 1
                merge[c, r, j * B + c * R + r] = 1
    spread = jnp.asarray(gather.transpose(0, 2, 1), BF16)
    gather, merge = jnp.asarray(gather, BF16), jnp.asarray(merge, BF16)

    q16 = query_rows[0].reshape(R, Q, DQ).transpose(1, 0, 2).reshape(B, DQ)
    rows = jnp.concatenate(
        [
            resid_rows[0].astype(F32),
            norm_gain.astype(F32)[None],
            score_weight.astype(F32)[None],
            jnp.zeros((8 - R - 2, D), F32),
        ],
        axis=0,
    )
    rt = jnp.concatenate(
        [router_weight.T, score_weight[None], jnp.zeros((16 - E - 1, D), BF16)], axis=0
    )

    stages = E.bit_length() - 1
    climbs = stages + S.bit_length() - 1
    sems = 8 * (S - 1) + 2 * Q * (E - 1) + stages + climbs
    vmem, smem, hbm = (
        pl.BlockSpec(memory_space=pltpu.VMEM),
        pl.BlockSpec(memory_space=pltpu.SMEM),
        pl.BlockSpec(memory_space=pl.ANY),
    )
    blocks = pltpu.VMEM((S * B, DQ), BF16)
    loss, gquery, gresid, gkeys, gvalues = pl.pallas_call(
        functools.partial(kernel, (S, E, R, D, H, TOK, F, Q)),
        out_shape=(
            jax.ShapeDtypeStruct((8, 128), F32),
            jax.ShapeDtypeStruct((1, R, D), F32),
            jax.ShapeDtypeStruct((1, R, D), F32),
            jax.ShapeDtypeStruct((1, TOK, D), BF16),
            jax.ShapeDtypeStruct((1, TOK, D), BF16),
        ),
        in_specs=[vmem] * 5 + [smem] * 4 + [vmem] * 4 + [hbm] * 3,
        out_specs=(vmem,) * 5,
        scratch_shapes=[
            pltpu.VMEM((D, 2 * F), BF16),
            pltpu.VMEM((F, D), BF16),
            blocks,
            pltpu.VMEM((S * 8, 128), F32),
            blocks,
            blocks,
            blocks,
            pltpu.VMEM((S * 8, NR), F32),
            pltpu.VMEM((2 * stages, 8, NR), F32),
            pltpu.VMEM((Q, NR, DQ), BF16),
            pltpu.VMEM((NR, 2 * F), F32),
            pltpu.VMEM((NR, 2 * F), BF16),
            pltpu.VMEM((NR, F), BF16),
            pltpu.VMEM((16, F), F32),
            pltpu.VMEM((Q, NR, DQ), BF16),
            pltpu.VMEM((Q, NR - SR, DQ), BF16),
            pltpu.VMEM((Q, NR - SR, DQ), BF16),
            pltpu.VMEM((climbs, 8, NR), F32),
            pltpu.VMEM((climbs, 8, NR), F32),
            blocks,
            blocks,
            blocks,
            blocks,
            blocks,
            pltpu.VMEM((SR, D), F32),
            pltpu.VMEM((SR, D), F32),
            pltpu.VMEM((SR, D), F32),
            pltpu.VMEM((H // group, group * SR, TOK), F32),
            pltpu.VMEM((H // group, group * SR, TOK), BF16),
            pltpu.SemaphoreType.DMA((sems,)),
            pltpu.SemaphoreType.DMA((sems,)),
            pltpu.SemaphoreType.DMA((3,)),
        ],
        compiler_params=pltpu.CompilerParams(
            collective_id=0, has_side_effects=True, vmem_limit_bytes=60 * 1024 * 1024
        ),
    )(
        q16,
        rows,
        key_rows,
        value_rows,
        log_decay,
        read_pos,
        expert_ids,
        pair_order,
        lengths,
        rt,
        gather,
        spread,
        merge,
        gate_weight,
        up_weight,
        down_weight,
    )
    return loss[0, 0], gquery, gresid, gkeys, gvalues


def solution(mesh):
    in_specs = (
        P("exp", "seq", None),
        P("exp", "seq", None),
        P("exp", "seq", None),
        P("exp", "seq", None),
        P("exp", None, "seq"),
        P("exp", "seq"),
        P("exp", "seq", None),
        P(),
        P(),
        P(),
        P(),
        P(),
        P("exp", None, "seq"),
        P("exp", None, "seq"),
        P("exp", "seq", None),
    )
    out_specs = (
        P(),
        P("exp", "seq", None),
        P("exp", "seq", None),
        P("exp", "seq", None),
        P("exp", "seq", None),
    )
    return jax.shard_map(
        per_device, mesh=mesh, in_specs=in_specs, out_specs=out_specs, check_vma=False
    )
```

```python
import functools

import jax
import jax.numpy as jnp
import numpy as np
from jax import lax
from jax.experimental import pallas as pl
from jax.experimental.pallas import tpu as pltpu
from jax.sharding import PartitionSpec as P

EPSILON = 1e-06
LENGTH_WEIGHT = 4.0
SCORE_SCALE = 256.0
NEGATIVE = -1e30
PARTS = 2
MESH = pl.DeviceIdType.MESH
F32 = jnp.float32
BF16 = jnp.bfloat16


def nt(a, b, **kw):
    return lax.dot_general(a, b, (((1,), (1,)), ((), ())), preferred_element_type=F32, **kw)


def tn(a, b):
    return lax.dot_general(a, b, (((0,), (0,)), ((), ())), preferred_element_type=F32)


def nn(a, b, **kw):
    return lax.dot_general(a, b, (((1,), (0,)), ((), ())), preferred_element_type=F32, **kw)


def iota(shape, dim):
    return lax.broadcasted_iota(jnp.int32, shape, dim)


def lane_sum(x):
    return jnp.sum(x, axis=1, keepdims=True)


def row_sum(x):
    return jnp.sum(x, axis=0, keepdims=True)


def tile_size(count, best):
    while count % best:
        best //= 2
    return best


def kernel(
    dims,
    query_ref,
    resid_ref,
    key_ref,
    value_ref,
    decay_ref,
    pos_ref,
    ids_ref,
    order_ref,
    length_ref,
    gain_ref,
    router_ref,
    score_ref,
    gather_ref,
    spread_ref,
    merge_ref,
    gate_hbm,
    up_hbm,
    down_hbm,
    loss_ref,
    gquery_ref,
    gresid_ref,
    gkeys_ref,
    gvalues_ref,
    w_buf,
    down_buf,
    q_buf,
    info_buf,
    att_send,
    att_recv,
    n_buf,
    meta_buf,
    meta_exp,
    x_buf,
    acc,
    h_buf,
    act_buf,
    v_buf,
    u_buf,
    red_recv,
    red_sum,
    t_send,
    t_recv,
    seq_send,
    seq_recv,
    d_buf,
    gq_send,
    gq_recv,
    pad_query,
    pad_resid,
    pad_router,
    rt_ref,
    pulled_scr,
    qn,
    dn,
    natural,
    w_scr,
    g_scr,
    send_sem,
    recv_sem,
    load_sem,
):
    S, E, R, D, H, TOK, F, Q = dims
    DQ, SR = D // Q, S * R
    DH = D // PARTS
    DP = DH // Q
    NR = E * SR
    HD = D // H
    B = R * Q
    seq, exp = lax.axis_index("seq"), lax.axis_index("exp")
    seq_bits = [1 << b for b in range(S.bit_length() - 1)]
    exp_bits = [1 << b for b in range(E.bit_length() - 1)]
    used = [0]
    sent = []

    def flip(me, bit):
        return me + bit * (1 - 2 * ((me // bit) % 2))

    def push(src, dst, device):
        k = used[0]
        used[0] += 1
        copy = pltpu.make_async_remote_copy(
            src_ref=src,
            dst_ref=dst,
            send_sem=send_sem.at[k],
            recv_sem=recv_sem.at[k],
            device_id=device,
            device_id_type=MESH,
        )
        copy.start()
        sent.append(copy)
        return copy

    def rows_of(index, size):
        return pl.ds(pl.multiple_of(index * size, size), size)

    def share(buf, size):
        out = []
        if size == B:
            return [share_part(buf, h) for h in range(PARTS)]
        for k in range(1, S):
            piece = buf.at[rows_of(seq, size)]
            out.append(push(piece, piece, (lax.rem(seq + k, S), exp)))
        return out

    def share_part(buf, h):
        out = []
        for k in range(1, S):
            piece = buf.at[h, rows_of(seq, B)]
            out.append(push(piece, piece, (lax.rem(seq + k, S), exp)))
        return out

    def scatter(src, dst, h):
        out = []
        for k in range(1, S):
            to = lax.rem(seq + k, S)
            out.append(push(src.at[h, rows_of(to, B)], dst.at[h, rows_of(seq, B)], (to, exp)))
        dst[h, rows_of(seq, B), :] = src[h, rows_of(seq, B), :]
        return out

    pick = iota((B, 16), 0) - iota((B, 16), 1)
    low = iota((B, 16), 1) < R
    picks = [((pick == c * R) & low).astype(BF16) for c in range(Q)]

    def own_blocks(rows, buf):
        for h in range(PARTS):
            block = jnp.zeros((B, DP), F32)
            for c in range(Q):
                at = h * DH + c * DP
                block = block + nn(picks[c], rows[:, at : at + DP])
            buf[h, rows_of(seq, B), :] = block.astype(BF16)

    def to_blocks(read, dst, h):
        out = jnp.zeros((S * B, DP), F32)
        for c in range(Q):
            at = h * DH + c * DP
            out = out + nn(spread_ref[c], read(slice(at, at + DP)).astype(BF16))
        dst[h] = out.astype(BF16)

    def from_blocks(buf, h):
        return jnp.concatenate([nn(merge_ref[c], buf[h]) for c in range(Q)], axis=1)

    def unpack(buf, dst, h):
        for c in range(Q):
            at = h * DH + c * DP
            dst[:, at : at + DP] = nn(gather_ref[c], buf[h])

    def arrive(copies):
        for copy in copies:
            copy.wait_recv()

    loads = [
        pltpu.make_async_copy(down_hbm.at[0], down_buf, load_sem.at[0]),
        pltpu.make_async_copy(gate_hbm.at[0], w_buf.at[:, pl.ds(0, F)], load_sem.at[1]),
        pltpu.make_async_copy(up_hbm.at[0], w_buf.at[:, pl.ds(F, F)], load_sem.at[2]),
    ]
    for load in loads:
        load.start()

    barrier = pltpu.get_barrier_semaphore()
    peers = [(lax.rem(seq + k, S), exp) for k in range(1, S)]
    peers += [(seq, flip(exp, bit)) for bit in exp_bits]
    for peer in peers:
        pl.semaphore_signal(barrier, inc=1, device_id=peer, device_id_type=MESH)

    for ref in (pad_query, pad_resid, pad_router):
        ref[...] = jnp.zeros(ref.shape, F32)
    pad_query[0:R, :] = query_ref[0].astype(F32)
    pad_resid[0:R, :] = resid_ref[0].astype(F32)
    gain = gain_ref[...].astype(F32).reshape(1, D)
    score_w = score_ref[...].astype(F32).reshape(1, D)
    pad_router[0:E, :] = router_ref[...].astype(F32)
    pad_router[E : E + 1, :] = score_w
    rt_ref[...] = pad_router[...].astype(BF16)
    upper = (iota((TOK, TOK), 0) <= iota((TOK, TOK), 1)).astype(F32)
    cum = nn(decay_ref[0], upper, precision=lax.Precision.HIGHEST)
    sub8, lane8 = iota((8, TOK), 0), iota((8, TOK), 1)
    place = jnp.full((8, TOK), TOK - 1, jnp.int32)
    for r in range(R):
        place = jnp.where(sub8 == r, pos_ref[0, r] - seq * TOK, place)
    hot = (lane8 == place).astype(F32)
    marks = nt(hot, cum, precision=lax.Precision.HIGHEST)
    info_buf[rows_of(seq, 8), :] = jnp.zeros((8, 128), F32)
    info_buf[rows_of(seq, 8), 0:H] = marks
    own_blocks(pad_query[...].astype(BF16), q_buf)

    pl.semaphore_wait(barrier, len(peers))
    info_copies = share(info_buf, 8)
    q_copies = share(q_buf, B)

    loads[0].wait()
    step = tile_size(F, 128)

    def project(i, carry):
        at = pl.multiple_of(i * step, step)
        v_buf[:, pl.ds(at, step)] = nt(rt_ref[...], down_buf[pl.ds(at, step), :])
        return carry

    lax.fori_loop(0, F // step, project, 0)

    arrive(info_copies)
    total = jnp.zeros((1, 128), F32)
    parts, masks = [], []
    lane_r, sub_r = iota((R, TOK), 1), iota((R, TOK), 0)
    own_place = jnp.zeros((R, TOK), jnp.int32)
    for r in range(R):
        own_place = jnp.where(sub_r == r, pos_ref[0, r] - seq * TOK, own_place)
    own_mask = jnp.where(lane_r <= own_place, 0.0, NEGATIVE)
    for j in range(S):
        block = info_buf[j * 8 : (j + 1) * 8, :]
        parts.append(block[0:R] + total)
        masks.append(jnp.where(j == seq, own_mask, jnp.where(j > seq, 0.0, NEGATIVE)))
        total = total + jnp.where(j >= seq, block[R : R + 1], 0.0)
    lifted = jnp.concatenate(parts, axis=0)
    mask = jnp.concatenate(masks, axis=0)

    group = 128 // HD
    lane = iota((SR, 128), 1)
    slots = [((lane >= g * HD) & (lane < (g + 1) * HD)) for g in range(group)]

    def stacked(x):
        return jnp.concatenate([jnp.where(s, x, 0.0) for s in slots], axis=0).astype(BF16)

    def chosen_lanes(x):
        out = x[0:SR]
        for g in range(1, group):
            out = jnp.where(slots[g], x[g * SR : (g + 1) * SR], out)
        return out

    heads = H // group // PARTS
    for p in range(H // group):
        w_scr[p] = jnp.concatenate(
            [
                jnp.exp(lifted[:, h : h + 1] - cum[h : h + 1, :] + mask)
                for h in range(p * group, (p + 1) * group)
            ],
            axis=0,
        )

    att_copies = []
    for part in range(PARTS):
        arrive(q_copies[part])
        unpack(q_buf, qn, part)
        for p in range(part * heads, (part + 1) * heads):
            at = slice(p * 128, (p + 1) * 128)
            qk = nt(stacked(qn[:, at]), key_ref[0, :, at]) * (1.0 / HD)
            mixed = (w_scr[p] * qk).astype(BF16)
            g_scr[p] = mixed
            natural[:, at] = chosen_lanes(nn(mixed, value_ref[0, :, at]))
        to_blocks(lambda at: natural[:, at], att_send, part)
        att_copies.append(scatter(att_send, att_recv, part))

    attended = []
    for part in range(PARTS):
        arrive(att_copies[part])
        attended.append(from_blocks(att_recv, part))
    attended = jnp.concatenate(attended, axis=1)
    live = iota((8, 1), 0) < R
    residual = jnp.where(live, pad_resid[...] + attended, 0.0)
    inverse = lax.rsqrt(lane_sum(residual * residual) * (1.0 / D) + EPSILON)
    unit = residual * inverse
    normed = jnp.concatenate([unit * gain, jnp.zeros((8, D), F32)], axis=0).astype(BF16)
    own_blocks(normed, n_buf)
    n_copies = share(n_buf, B)

    logits = nt(normed, rt_ref[...])[0:8]
    sub_l, lane_l = iota((8, 16), 0), iota((8, 16), 1)
    sub_n, lane_n = iota((8, NR), 0), iota((8, NR), 1)
    own_lane = (exp * S + seq) * R
    id0 = jnp.full((8, 16), -1, jnp.int32)
    id1 = jnp.full((8, 16), -1, jnp.int32)
    meta = jnp.zeros((8, NR), F32)
    for r in range(R):
        id0 = jnp.where(sub_l == r, ids_ref[0, 0, r], id0)
        id1 = jnp.where(sub_l == r, ids_ref[0, 1, r], id1)
        here = lane_n == own_lane + r
        meta = jnp.where(here & (sub_n == 0), ids_ref[0, 0, r].astype(F32), meta)
        meta = jnp.where(here & (sub_n == 1), ids_ref[0, 1, r].astype(F32), meta)
    difference = (lane_l == id0).astype(F32) - (lane_l == id1).astype(F32)
    first_own = jax.nn.sigmoid(lane_sum(difference * logits))
    base_own = lane_sum(residual * score_w)
    own_hot = (lane_n == own_lane + sub_n) & (sub_n < R)
    meta = meta + jnp.where(sub_n == 2, row_sum(jnp.where(own_hot, base_own, 0.0)), 0.0)
    meta = meta + jnp.where(sub_n == 3, row_sum(jnp.where(own_hot, first_own, 0.0)), 0.0)
    meta_buf[rows_of(seq, 8), :] = meta
    meta_copies = share(meta_buf, 8)

    downward = exp_bits[::-1]

    def spread_stage(c, bit):
        held = exp % (2 * bit)
        out = []
        for m in range(E // (2 * bit)):
            piece = x_buf.at[c, rows_of(held + m * 2 * bit, SR)]
            out.append(push(piece, piece, (seq, flip(exp, bit))))
        return out

    stage = []
    per_part = DQ // DP
    for h in range(PARTS):
        arrive(n_copies[h])
        for k in range(Q // PARTS):
            c = h * (Q // PARTS) + k
            for i in range(per_part):
                x_buf[c, rows_of(exp, SR), i * DP : (i + 1) * DP] = nn(
                    gather_ref[k * per_part + i], n_buf[h]
                ).astype(BF16)
            stage.append(spread_stage(c, downward[0]))
    arrive(meta_copies)
    meta = meta_buf[0:8, :]
    for j in range(1, S):
        meta = meta + meta_buf[j * 8 : (j + 1) * 8, :]

    for bit in downward[1:]:
        following = []
        for c in range(Q):
            arrive(stage[c])
            following.append(spread_stage(c, bit))
        stage = following

    for i, bit in enumerate(downward):
        meta_exp[2 * i] = meta
        copy = push(meta_exp.at[2 * i], meta_exp.at[2 * i + 1], (seq, flip(exp, bit)))
        copy.wait_recv()
        meta = meta + meta_exp[2 * i + 1]

    loads[1].wait()
    loads[2].wait()
    wide = tile_size(2 * F, 768 if (2 * F) % 768 == 0 else 256)
    for c in range(Q):
        arrive(stage[c])

        def grow(i, carry, c=c):
            at = pl.ds(pl.multiple_of(i * wide, wide), wide)
            part = nn(x_buf[c], w_buf[c * DQ : (c + 1) * DQ, at])
            acc[:, at] = part if c == 0 else acc[:, at] + part
            return carry

        lax.fori_loop(0, 2 * F // wide, grow, 0)

    id0_all, id1_all = meta[0:1], meta[1:2]
    base_all, first_all = meta[2:3], meta[3:4]
    mine = exp.astype(F32)
    gate_row = jnp.where(id0_all == mine, first_all, 0.0) + jnp.where(
        id1_all == mine, 1.0 - first_all, 0.0
    )
    v = v_buf[E : E + 1, :]
    sub16, lane16 = iota((16, NR), 0), iota((16, NR), 1)

    def activate(i, carry):
        at = pl.ds(pl.multiple_of(i * 16, 16), 16)
        gate = lane_sum(jnp.where(lane16 == sub16 + i * 16, gate_row, 0.0))
        pre_gate = acc[at, 0:F]
        pre_up = acc[at, F : 2 * F]
        sig = jax.nn.sigmoid(pre_gate)
        silu = pre_gate * sig
        act_buf[at, :] = (silu * pre_up).astype(BF16)
        gv = gate * v
        h_buf[at, 0:F] = (gv * pre_up * sig * (1.0 + pre_gate * (1.0 - sig))).astype(BF16)
        h_buf[at, F : 2 * F] = (gv * silu).astype(BF16)
        return carry

    lax.fori_loop(0, NR // 16, activate, 0)
    v_high = v.astype(BF16).astype(F32)
    sub_v = iota((16, F), 0)
    v_two = jnp.where(sub_v == 0, v_high, jnp.where(sub_v == 1, v - v_high, 0.0)).astype(BF16)
    own_t = row_sum(nt(v_two, act_buf[...]))
    table = jnp.where(sub_n == exp, own_t, 0.0)

    ladder = [(seq, flip(exp, bit)) for bit in exp_bits]
    ladder += [(flip(seq, bit), exp) for bit in seq_bits]
    climb = []

    def climb_start(table):
        i = len(climb)
        t_send[i] = table
        climb.append(push(t_send.at[i], t_recv.at[i], ladder[i]))

    def climb_end(table):
        i = len(climb) - 1
        climb[i].wait_recv()
        return table + t_recv[i]

    offsets, count = [], E
    reach = 0
    for bit in exp_bits:
        offsets.append(reach)
        count //= 2
        reach += count * SR

    def held_rows(i, m):
        return u_buf, m * SR if i == 0 else offsets[i - 1] + m * SR

    def fold_start(c, i):
        bit = exp_bits[i]
        side = 1 - (exp // bit) % 2
        out = []
        for m in range(E // (2 * bit)):
            if i == 0:
                src = u_buf.at[c, rows_of(2 * m + side, SR)]
            else:
                src = red_sum.at[c, rows_of(offsets[i - 1] // SR + 2 * m + side, SR)]
            dst = red_recv.at[c, pl.ds(offsets[i] + m * SR, SR)]
            out.append(push(src, dst, (seq, flip(exp, bit))))
        return out

    def fold_end(c, i, copies):
        bit = exp_bits[i]
        side = (exp // bit) % 2
        for m, copy in enumerate(copies):
            copy.wait_recv()
            if i == 0:
                own = u_buf[c, rows_of(2 * m + side, SR), :]
            else:
                own = red_sum[c, rows_of(offsets[i - 1] // SR + 2 * m + side, SR), :]
            at = pl.ds(offsets[i] + m * SR, SR)
            red_sum[c, at, :] = (own.astype(F32) + red_recv[c, at, :].astype(F32)).astype(BF16)

    deep = tile_size(DQ, 256)
    folds = {}
    for c in range(Q):
        if c < len(ladder):
            climb_start(table)

        def back(i, carry, c=c):
            at = pl.multiple_of(i * deep, deep)
            u_buf[c, :, pl.ds(at, deep)] = nt(
                h_buf[...], w_buf[pl.ds(c * DQ + at, deep), :]
            ).astype(BF16)
            return carry

        lax.fori_loop(0, DQ // deep, back, 0)
        folds[c, 0] = fold_start(c, 0)
        if c >= 1:
            fold_end(c - 1, 0, folds[c - 1, 0])
            if len(exp_bits) > 1:
                folds[c - 1, 1] = fold_start(c - 1, 1)
        if c < len(ladder):
            table = climb_end(table)
    fold_end(Q - 1, 0, folds[Q - 1, 0])
    if len(exp_bits) > 1:
        folds[Q - 1, 1] = fold_start(Q - 1, 1)
    while len(climb) < len(ladder):
        climb_start(table)
        table = climb_end(table)

    low_e = iota((E, NR), 0).astype(F32)
    picked0 = row_sum(jnp.where(low_e == id0_all, table[0:E], 0.0))
    picked1 = row_sum(jnp.where(low_e == id1_all, table[0:E], 0.0))
    score = base_all + first_all * picked0 + (1.0 - first_all) * picked1
    in_seq = (lane_n >= sub_n * SR) & (lane_n < (sub_n + 1) * SR)
    rewards = lane_sum(jnp.where(in_seq, score, 0.0)) * (1.0 / SR)
    column = iota((8, 1), 0)
    d_reward = jnp.zeros((8, 1), F32)
    fitted = jnp.zeros((1, 1), F32)
    for pair in range(E // 2):
        best, worst = order_ref[2 * pair], order_ref[2 * pair + 1]
        gap = row_sum(
            jnp.where(column == worst, rewards, 0.0) - jnp.where(column == best, rewards, 0.0)
        )
        fitted = fitted + jnp.maximum(gap, 0.0) + jnp.log1p(jnp.exp(-jnp.abs(gap)))
        slope = jax.nn.sigmoid(gap) * (2.0 / E)
        d_reward = d_reward + jnp.where(column == worst, slope, 0.0)
        d_reward = d_reward - jnp.where(column == best, slope, 0.0)
    portion = jnp.zeros((8, 1), F32)
    for i in range(E):
        portion = jnp.where(column == i, length_ref[i].astype(F32) / (TOK * S), portion)
    real = column < E
    spread = jnp.where(real, portion - row_sum(portion) / E, 0.0)
    centred = jnp.where(real, rewards - row_sum(jnp.where(real, rewards, 0.0)) / E, 0.0)
    cov = row_sum(centred * spread) / E
    loss_ref[...] = fitted * (2.0 / E) + LENGTH_WEIGHT * cov * cov
    d_reward = d_reward + (2.0 * LENGTH_WEIGHT / E) * cov * spread
    own_grad = row_sum(jnp.where(column == exp, d_reward, 0.0)) * SCORE_SCALE
    d_logit_row = (picked0 - picked1) * first_all * (1.0 - first_all)
    d_logit = lane_sum(jnp.where(own_hot, d_logit_row, 0.0)) * own_grad

    last = pl.ds(offsets[-1], SR)
    copies = []
    for c in range(Q):
        for i in range(1, len(exp_bits)):
            fold_end(c, i, folds[c, i])
            if i + 1 < len(exp_bits):
                folds[c, i + 1] = fold_start(c, i + 1)
        if (c + 1) % (Q // PARTS) == 0:
            h = c // (Q // PARTS)

            def reduced(at):
                k = at.start // DQ
                return red_sum[k, last, at.start - k * DQ : at.stop - k * DQ]

            to_blocks(reduced, seq_send, h)
            copies.append(scatter(seq_send, seq_recv, h))
    columns = nn(
        jnp.concatenate([difference, jnp.zeros((8, 16), F32)], axis=0).astype(BF16), rt_ref[...]
    )[0:8]
    pieces = []
    for h in range(PARTS):
        arrive(copies[h])
        pieces.append(from_blocks(seq_recv, h))
    d_normed = own_grad * jnp.concatenate(pieces, axis=1) + d_logit * columns
    d_unit = d_normed * gain
    grad_resid = own_grad * score_w + inverse * (
        d_unit - unit * (lane_sum(d_unit * unit) * (1.0 / D))
    )
    grad_resid = jnp.where(live, grad_resid, 0.0)
    gresid_ref[0] = grad_resid[0:R]
    rounded = jnp.concatenate([grad_resid, jnp.zeros((8, D), F32)], axis=0).astype(BF16)
    own_blocks(rounded, d_buf)
    d_copies = share(d_buf, B)
    gq_copies = []
    for part in range(PARTS):
        arrive(d_copies[part])
        unpack(d_buf, dn, part)
        for p in range(part * heads, (part + 1) * heads):
            at = slice(p * 128, (p + 1) * 128)
            grad_dot = nt(stacked(dn[:, at]), value_ref[0, :, at]) * (1.0 / HD)
            pulled = (w_scr[p] * grad_dot).astype(BF16)
            pulled_scr[p] = pulled
            natural[:, at] = chosen_lanes(nn(pulled, key_ref[0, :, at]))
        to_blocks(lambda at: natural[:, at], gq_send, part)
        gq_copies.append(scatter(gq_send, gq_recv, part))
    for p in range(H // group):
        at = slice(p * 128, (p + 1) * 128)
        gkeys_ref[0, :, at] = tn(pulled_scr[p], stacked(qn[:, at])).astype(BF16)
        gvalues_ref[0, :, at] = tn(g_scr[p], stacked(dn[:, at])).astype(BF16)
    for part in range(PARTS):
        arrive(gq_copies[part])
        gquery_ref[0, :, part * DH : (part + 1) * DH] = from_blocks(gq_recv, part)[0:R]
    for copy in sent:
        copy.wait_send()


def hand_out(*refs):
    sems = refs[-1]
    copies = [
        pltpu.make_async_copy(src, dst, sems.at[i])
        for i, (src, dst) in enumerate(zip(refs[1:5], refs[6:10]))
    ]
    for copy in copies:
        copy.start()
    refs[5][...] = refs[0][...]
    for copy in copies:
        copy.wait()


def per_device(
    resid_rows,
    query_rows,
    key_rows,
    value_rows,
    log_decay,
    read_pos,
    expert_ids,
    pair_order,
    lengths,
    norm_gain,
    router_weight,
    score_weight,
    gate_weight,
    up_weight,
    down_weight,
):
    S, E = lax.axis_size("seq"), lax.axis_size("exp")
    _, R, D = query_rows.shape
    TOK, H = key_rows.shape[1], log_decay.shape[1]
    F = gate_weight.shape[2]
    extra = -F % 128
    if extra:
        gate_weight = jnp.pad(gate_weight, ((0, 0), (0, 0), (0, extra)))
        up_weight = jnp.pad(up_weight, ((0, 0), (0, 0), (0, extra)))
        down_weight = jnp.pad(down_weight, ((0, 0), (0, extra), (0, 0)))
        F += extra
    Q = 16 // R
    B, DQ, SR = R * Q, D // Q, S * R
    NR = E * SR
    group = 128 // (D // H)

    gather = np.zeros((Q, SR, S * B), np.float32)
    merge = np.zeros((Q, 8, S * B), np.float32)
    for c in range(Q):
        for j in range(S):
            for r in range(R):
                gather[c, j * R + r, j * B + c * R + r] = 1
                merge[c, r, j * B + c * R + r] = 1
    spread = jnp.asarray(gather.transpose(0, 2, 1), BF16)
    gather, merge = jnp.asarray(gather, BF16), jnp.asarray(merge, BF16)

    stages = E.bit_length() - 1
    climbs = stages + S.bit_length() - 1
    sems = (6 * PARTS + 2) * (S - 1) + 2 * Q * (E - 1) + stages + climbs
    vmem, smem, hbm = (
        pl.BlockSpec(memory_space=pltpu.VMEM),
        pl.BlockSpec(memory_space=pltpu.SMEM),
        pl.BlockSpec(memory_space=pl.ANY),
    )
    blocks = pltpu.VMEM((PARTS, S * B, D // PARTS // Q), BF16)
    results = pl.pallas_call(
        functools.partial(kernel, (S, E, R, D, H, TOK, F, Q)),
        out_shape=(
            jax.ShapeDtypeStruct((1, 1), F32),
            jax.ShapeDtypeStruct((1, R, D), F32),
            jax.ShapeDtypeStruct((1, R, D), F32),
            jax.ShapeDtypeStruct((1, TOK, D), BF16),
            jax.ShapeDtypeStruct((1, TOK, D), BF16),
        ),
        in_specs=[vmem] * 5 + [smem] * 4 + [vmem] * 6 + [hbm] * 3,
        out_specs=(vmem,) * 5,
        scratch_shapes=[
            pltpu.VMEM((D, 2 * F), BF16),
            pltpu.VMEM((F, D), BF16),
            blocks,
            pltpu.VMEM((S * 8, 128), F32),
            blocks,
            blocks,
            blocks,
            pltpu.VMEM((S * 8, NR), F32),
            pltpu.VMEM((2 * stages, 8, NR), F32),
            pltpu.VMEM((Q, NR, DQ), BF16),
            pltpu.VMEM((NR, 2 * F), F32),
            pltpu.VMEM((NR, 2 * F), BF16),
            pltpu.VMEM((NR, F), BF16),
            pltpu.VMEM((16, F), F32),
            pltpu.VMEM((Q, NR, DQ), BF16),
            pltpu.VMEM((Q, NR - SR, DQ), BF16),
            pltpu.VMEM((Q, NR - SR, DQ), BF16),
            pltpu.VMEM((climbs, 8, NR), F32),
            pltpu.VMEM((climbs, 8, NR), F32),
            blocks,
            blocks,
            blocks,
            blocks,
            blocks,
            pltpu.VMEM((16, D), F32),
            pltpu.VMEM((8, D), F32),
            pltpu.VMEM((16, D), F32),
            pltpu.VMEM((16, D), BF16),
            pltpu.VMEM((H // group, group * SR, TOK), BF16),
            pltpu.VMEM((SR, D), F32),
            pltpu.VMEM((SR, D), F32),
            pltpu.VMEM((SR, D), F32),
            pltpu.VMEM((H // group, group * SR, TOK), F32),
            pltpu.VMEM((H // group, group * SR, TOK), BF16),
            pltpu.SemaphoreType.DMA((sems,)),
            pltpu.SemaphoreType.DMA((sems,)),
            pltpu.SemaphoreType.DMA((3,)),
        ],
        compiler_params=pltpu.CompilerParams(
            collective_id=0, has_side_effects=True, vmem_limit_bytes=60 * 1024 * 1024
        ),
    )(
        query_rows,
        resid_rows,
        key_rows,
        value_rows,
        log_decay,
        read_pos,
        expert_ids.transpose(0, 2, 1),
        pair_order,
        lengths,
        norm_gain,
        router_weight.T,
        score_weight,
        gather,
        spread,
        merge,
        gate_weight,
        up_weight,
        down_weight,
    )
    moved = pl.pallas_call(
        hand_out,
        out_shape=tuple(jax.ShapeDtypeStruct(x.shape, x.dtype) for x in results),
        in_specs=[vmem] + [hbm] * 4,
        out_specs=(vmem,) + (hbm,) * 4,
        scratch_shapes=[pltpu.SemaphoreType.DMA((4,))],
    )(*results)
    return (moved[0].reshape(()),) + tuple(moved[1:])


def solution(mesh):
    in_specs = (
        P("exp", "seq", None),
        P("exp", "seq", None),
        P("exp", "seq", None),
        P("exp", "seq", None),
        P("exp", None, "seq"),
        P("exp", "seq"),
        P("exp", "seq", None),
        P(),
        P(),
        P(),
        P(),
        P(),
        P("exp", None, "seq"),
        P("exp", None, "seq"),
        P("exp", "seq", None),
    )
    out_specs = (
        P(),
        P("exp", "seq", None),
        P("exp", "seq", None),
        P("exp", "seq", None),
        P("exp", "seq", None),
    )
    return jax.shard_map(
        per_device, mesh=mesh, in_specs=in_specs, out_specs=out_specs, check_vma=False
    )
```
